256 devices in a mesh: shot: 16 (over y, x), space: 16 (over z, core).
Axes of the slice: x: 4, y: 4, z: 8, core: 2. Of those that a mesh axis runs over, the one named last changes fastest.
Arguments:
- right_side: float32 [2, 256, 16, 16, 16, 128], P(None, 'shot', 'space'), may hold values from -6 to 6
- wavenumber_sq: float32 [16, 16, 16, 128], P('space'), may hold values from 0.2 to 1.2
- source_cell: int32 [256], P('shot'), may hold values from 0 to 524287
- source_amplitude: float32 [2, 256], P(None, 'shot'), may hold values from -16 to 16
Outputs:
- wavefield: float32 [2, 256, 16, 16, 16, 128], P(None, 'shot', 'space')
The draws below stay inside these ranges and needn't reach their ends.
All inputs are finite; a program needn't handle non-finite values.
Results may differ from the reference program's by a relative error of at most 0.0003.
Values sent between devices are 32-bit elements; how exact they have to be, the bound alone decides.
No kernel may reach another device: no remote copies, remote signals or barrier semaphores. Data moves between devices by JAX's collectives and lax.ppermute only.
A program may use at most 128 MiB of HBM per device.

```python
import math
import jax
import jax.numpy as jnp
from jax import lax

BLOCK = 16
CZ = 128
TY = 4
PRE = 2
COARSE = 4
POST = 1
TILES = 16
SHOTS = 256
NX = 64
NY = 64


def draw_right_side(key, part):
    key = jax.random.fold_in(key, 11)
    shape = (2, SHOTS, TILES, BLOCK, BLOCK, CZ)
    rough = jax.random.normal(key, shape, jnp.float32)
    values = rough
    return jnp.clip(values, -6.0, 6.0)


def set_ends(values, key, least, high):
    longest = values.shape.index(max(values.shape))
    spots = []
    for shift in (0, 1):
        where = [jax.random.randint(jax.random.fold_in(key, axis), (), 0, length) for axis, length in enumerate(values.shape)]
        where[longest] = (where[longest] + shift) % values.shape[longest]
        spots.append(tuple(where))
    return values.at[spots[0]].set(least).at[spots[1]].set(high)


def steps_of(stream_key, dims, cuts, low, top_value):
    level = 1.0
    for dim, blocks in cuts:
        steps = jax.random.uniform(jax.random.fold_in(jax.random.fold_in(stream_key, 6), dim), (blocks,), jnp.float32, low / len(cuts), top_value / len(cuts))
        level = level * jnp.repeat(jnp.exp(steps), dims[dim] // blocks).reshape((-1,) + (1,) * (len(dims) - 1 - dim))
    return level


def scatter_about(key, shape, scale, bound, split=(), held_as=jnp.bfloat16):
    values = jax.random.normal(key, shape, jnp.float32) * scale
    if len(split) > 0:
        values = steps_of(key, shape, split, -0.22, 0.18) * values
    return jnp.clip(values, min=-bound, max=bound).astype(held_as)


def setup_inputs(seed: int = 0) -> dict:
    key_list = jax.random.split(jax.random.key(seed), 5)
    right_side = draw_right_side(jax.random.fold_in(key_list[4], 71), 0)
    wavenumber_sq = jnp.clip(jnp.exp(math.log(1.2) - 1.7917595 * jax.random.uniform(key_list[1], (TILES, BLOCK, BLOCK, CZ), jnp.float32) ** steps_of(key_list[1], (TILES, BLOCK, BLOCK, CZ), ((0, 16),), -0.2, 0.2)), 0.2, 1.2)
    source_cell = set_ends(jax.random.randint(key_list[2], (SHOTS,), 0, NX * NY * CZ), jax.random.fold_in(key_list[2], 1), 0, (NX * NY * CZ) - 1).astype(jnp.int32)
    source_amplitude = scatter_about(key_list[3], (2, SHOTS), 4.0, 16.0, ((1, 16),), jnp.float32)
    return {"right_side": right_side, "wavenumber_sq": wavenumber_sq, "source_cell": source_cell, "source_amplitude": source_amplitude}


OMEGA = 0.8
BETA = 0.5


def inverse_diag(diag_r, diag_i):
    scale = 1.0 / (diag_r * diag_r + diag_i * diag_i)
    return diag_r * scale, -diag_i * scale


def tile_perm(count):
    return tuple(range(count)) + (count, count + 2, count + 1, count + 3, count + 4)


def to_grid(tiles):
    lead = tiles.shape[:-4]
    count, size_x, size_y, depth = tiles.shape[-4:]
    rows = count // TY
    shaped = tiles.reshape(lead + (rows, TY, size_x, size_y, depth))
    return shaped.transpose(tile_perm(len(lead))).reshape(lead + (rows * size_x, TY * size_y, depth))


def to_tiles(grid, size_x, size_y):
    lead = grid.shape[:-3]
    width_x, width_y, depth = grid.shape[-3:]
    rows = width_x // size_x
    cols = width_y // size_y
    shaped = grid.reshape(lead + (rows, size_x, cols, size_y, depth))
    return shaped.transpose(tile_perm(len(lead))).reshape(lead + (rows * cols, size_x, size_y, depth))


def coarsen(field):
    lead = field.shape[:-3]
    width_x, width_y, depth = field.shape[-3:]
    shaped = field.reshape(lead + (width_x // 2, 2, width_y // 2, 2, depth))
    total = shaped[..., :, 0, :, 0, :] + shaped[..., :, 1, :, 0, :]
    total = total + shaped[..., :, 0, :, 1, :] + shaped[..., :, 1, :, 1, :]
    return 0.25 * total


def refine(field):
    return jnp.repeat(jnp.repeat(field, 2, axis=-3), 2, axis=-2)


def grid_operator(field, diag_r, diag_i, weight_x):
    widths = ((0, 0),) * (field.ndim - 3) + ((1, 1),) * 3
    padded = jnp.pad(field, widths)
    along_x = padded[..., 2:, 1:-1, 1:-1] + padded[..., :-2, 1:-1, 1:-1]
    along_y = padded[..., 1:-1, 2:, 1:-1] + padded[..., 1:-1, :-2, 1:-1]
    along_z = padded[..., 1:-1, 1:-1, 2:] + padded[..., 1:-1, 1:-1, :-2]
    near = weight_x * (along_x + along_y) + along_z
    real = diag_r * field[0] - diag_i * field[1] - near[0]
    imag = diag_r * field[1] + diag_i * field[0] - near[1]
    return jnp.stack([real, imag])


def relax(field, rhs, image, inv_r, inv_i):
    rest_r = rhs[0] - image[0]
    rest_i = rhs[1] - image[1]
    real = field[0] + OMEGA * (inv_r * rest_r - inv_i * rest_i)
    imag = field[1] + OMEGA * (inv_r * rest_i + inv_i * rest_r)
    return jnp.stack([real, imag])


def reference(right_side, wavenumber_sq, source_cell, source_amplitude):
    k_fine = to_grid(wavenumber_sq)
    fine_r = 6.0 - k_fine
    fine_i = BETA * k_fine
    inv_r, inv_i = inverse_diag(fine_r, fine_i)
    k_coarse = coarsen(k_fine)
    coarse_r = 3.0 - k_coarse
    coarse_i = BETA * k_coarse
    cinv_r, cinv_i = inverse_diag(coarse_r, coarse_i)
    width_x, width_y, depth = k_fine.shape
    size_x, size_y = wavenumber_sq.shape[1], wavenumber_sq.shape[2]
    index_x = jnp.arange(width_x, dtype=jnp.int32)
    index_y = jnp.arange(width_y, dtype=jnp.int32)
    index_z = jnp.arange(depth, dtype=jnp.int32)

    def one_shot(items):
        tiles, cell, amplitude = items
        grid_x = cell // (width_y * depth)
        grid_y = (cell // depth) % width_y
        grid_z = cell % depth
        hit_x = (index_x == grid_x).astype(jnp.float32)
        hit_y = (index_y == grid_y).astype(jnp.float32)
        hit_z = (index_z == grid_z).astype(jnp.float32)
        hit = hit_x[:, None, None] * hit_y[None, :, None] * hit_z[None, None, :]
        rhs = to_grid(tiles) + amplitude[:, None, None, None] * hit[None]
        empty = jnp.zeros_like(rhs)
        field = relax(empty, rhs, empty, inv_r, inv_i)
        for sweep in range(PRE - 1):
            field = relax(field, rhs, grid_operator(field, fine_r, fine_i, 1.0), inv_r, inv_i)
        rest = rhs - grid_operator(field, fine_r, fine_i, 1.0)
        coarse_rhs = coarsen(rest)
        empty_c = jnp.zeros_like(coarse_rhs)
        corr = relax(empty_c, coarse_rhs, empty_c, cinv_r, cinv_i)
        for sweep in range(COARSE - 1):
            corr = relax(corr, coarse_rhs, grid_operator(corr, coarse_r, coarse_i, 0.25), cinv_r, cinv_i)
        field = field + refine(corr)
        for sweep in range(POST):
            field = relax(field, rhs, grid_operator(field, fine_r, fine_i, 1.0), inv_r, inv_i)
        return to_tiles(field, size_x, size_y)

    shots_first = jnp.moveaxis(right_side, 1, 0)
    amplitudes = jnp.moveaxis(source_amplitude, 1, 0)
    result = lax.map(one_shot, (shots_first, source_cell, amplitudes))
    return jnp.moveaxis(result, 0, 1)
```

```python
import functools

import jax
import jax.numpy as jnp
from jax import lax
from jax.experimental import pallas as pl
from jax.experimental.pallas import tpu as pltpu
from jax.sharding import PartitionSpec as P

TY = 4
OMEGA = 0.8
BETA = 0.5
B = 16
C = 8
Z = 128
F32 = jnp.float32
UNROLL = 4
PARTS = 2
FACE_STRIDE = 2 * B + 8
STRIDE = B * B + 8
Y_COUNT = (14, 12, 10, 8)
Y_START = (0, 14, 26, 36)


def z_sum(u):
    lane = lax.broadcasted_iota(jnp.int32, u.shape, 1)
    low = jnp.where(lane == 0, 0.0, pltpu.roll(u, 1, 1))
    high = jnp.where(lane == Z - 1, 0.0, pltpu.roll(u, Z - 1, 1))
    return low + high


def weight(k, centre):
    real = centre - k
    imag = BETA * k
    scale = jnp.where(k > 0.0, OMEGA / (real * real + imag * imag), 0.0)
    return real * scale, -imag * scale


def times(w_r, w_i, r, i):
    return w_r * r - w_i * i, w_r * i + w_i * r


def row_of(ref, c, x, y, shots):
    return jnp.broadcast_to(ref[c, x, pl.ds(y, 1), :], (shots, Z))


def sides_of(ref, c, x, y):
    return (ref[c, x - 1, y] + ref[c, x + 1, y]) + (ref[c, x, y - 1] + ref[c, x, y + 1])


def near(ref, cells):
    along = [z_sum(ref[c, x, y]) for x, y in cells for c in range(2)]
    return [[along[2 * n + c] + sides_of(ref, c, x, y) for c in range(2)] for n, (x, y) in enumerate(cells)]


def place():
    tile = lax.axis_index("space")
    return tile // TY, tile % TY


def sources(cell_ref, amp_ref, start, shots):
    sub = lax.broadcasted_iota(jnp.int32, (shots, Z), 0)
    lane = lax.broadcasted_iota(jnp.int32, (shots, Z), 1)
    cell = jnp.zeros((shots, Z), jnp.int32)
    amp_r = jnp.zeros((shots, Z), F32)
    amp_i = jnp.zeros((shots, Z), F32)
    for s in range(shots):
        cell = jnp.where(sub == s, cell_ref[start + s], cell)
        amp_r = jnp.where(sub == s, amp_ref[0, start + s], amp_r)
        amp_i = jnp.where(sub == s, amp_ref[1, start + s], amp_i)
    return cell - lane, amp_r, amp_i


def with_source(source, row, column, x, y, r, i):
    spot, amp_r, amp_i = source
    hit = spot == ((row * B + x) * (TY * B) + column * B + y) * Z
    return r + jnp.where(hit, amp_r, 0.0), i + jnp.where(hit, amp_i, 0.0)


def coarse_k(k2_ref, x):
    total = k2_ref[2 * x, pl.ds(0, C, stride=2), :] + k2_ref[2 * x + 1, pl.ds(0, C, stride=2), :]
    total = total + k2_ref[2 * x, pl.ds(1, C, stride=2), :] + k2_ref[2 * x + 1, pl.ds(1, C, stride=2), :]
    return 0.25 * total


def start_all(copies):
    for copy in copies:
        copy.start()
    return copies


def small_copies(pairs, sems):
    return [pltpu.make_async_copy(source, target, sems.at[n]) for n, (source, target) in enumerate(pairs)]


def faces_kernel(start, shots, cell_in, amp_in, raw_ref, k2_in, x0_ref, x1_ref, cell_ref, amp_ref, k2_ref, low_ref, high_ref, sems):
    width = 2 * B
    mine = pl.ds(start, shots)
    copies = small_copies(
        [
            (raw_ref.at[:, mine, pl.ds(0, width)], low_ref.at[:, :, pl.ds(0, width)]),
            (raw_ref.at[:, mine, pl.ds(B * B - width, width)], high_ref.at[:, :, pl.ds(0, width)]),
            (cell_in, cell_ref),
            (amp_in, amp_ref),
            (k2_in, k2_ref),
        ],
        sems,
    )
    for copy in start_all(copies):
        copy.wait()
    row, column = place()
    even = row % 2 == 0
    source = sources(cell_ref, amp_ref, start, shots)
    base = 64 * shots
    if start == 0:
        k_low, k_high = k2_ref[0], k2_ref[B - 1]
        x0_ref[pl.ds(base, B), :] = jnp.where(even, k_high, k_low)
        x1_ref[pl.ds(base, B), :] = jnp.where(even, k_low, k_high)
        for d in range(3):
            k_low, k_high = coarse_k(k2_ref, d), coarse_k(k2_ref, C - 1 - d)
            x0_ref[pl.ds(base + B + d * C, C), :] = jnp.where(even, k_high, k_low)
            x1_ref[pl.ds(base + B + d * C, C), :] = jnp.where(even, k_low, k_high)
    low = low_ref.reshape(2, shots * FACE_STRIDE, Z)
    high = high_ref.reshape(2, shots * FACE_STRIDE, Z)
    for d in range(2):
        lw_r, lw_i = weight(k2_ref[d], 6.0)
        hw_r, hw_i = weight(k2_ref[B - 1 - d], 6.0)
        for y in range(B):
            values = []
            for side, local, x, w_r, w_i in ((low, d, d, lw_r, lw_i), (high, 1 - d, B - 1 - d, hw_r, hw_i)):
                r, i = (side[c, pl.ds(local * B + y, shots, stride=FACE_STRIDE), :] for c in range(2))
                r, i = with_source(source, row, column, x, y, r, i)
                values.append(times(w_r[y : y + 1], w_i[y : y + 1], r, i))
            for c in range(2):
                at = pl.ds(((d * B + y) * 2 + c) * shots, shots)
                x0_ref[at, :] = jnp.where(even, values[1][c], values[0][c])
                x1_ref[at, :] = jnp.where(even, values[0][c], values[1][c])


def first_coarse(shots, v_ref, cb_ref, cw_ref, e_ref, cells):
    blocks, rings = [], []
    for x, y in cells:
        fx, fy = 2 * x + 1, 2 * y + 1
        for c in range(2):
            blocks.append((v_ref[c, fx, fy] + v_ref[c, fx + 1, fy]) + (v_ref[c, fx, fy + 1] + v_ref[c, fx + 1, fy + 1]))
            ring = (v_ref[c, fx - 1, fy] + v_ref[c, fx - 1, fy + 1]) + (v_ref[c, fx + 2, fy] + v_ref[c, fx + 2, fy + 1])
            rings.append(ring + (v_ref[c, fx, fy - 1] + v_ref[c, fx + 1, fy - 1]) + (v_ref[c, fx, fy + 2] + v_ref[c, fx + 1, fy + 2]))
    along = [z_sum(block) for block in blocks]
    for n, (x, y) in enumerate(cells):
        r, i = (cb_ref[c, x, y] + 0.25 * (2.0 * blocks[2 * n + c] + rings[2 * n + c] + along[2 * n + c]) for c in range(2))
        r, i = times(row_of(cw_ref, 0, x, y, shots), row_of(cw_ref, 1, x, y, shots), r, i)
        e_ref[0, x + 4, y + 4] = r
        e_ref[1, x + 4, y + 4] = i


def second_v(shots, u_ref, w_ref, v_ref, cells):
    sums = near(u_ref, [(x + 2, y + 2) for x, y in cells])
    for (x, y), (r, i) in zip(cells, sums):
        r, i = times(row_of(w_ref, 0, x + 1, y + 1, shots), row_of(w_ref, 1, x + 1, y + 1, shots), r, i)
        v_ref[0, x + 1, y + 1] = 0.4 * u_ref[0, x + 2, y + 2] + r
        v_ref[1, x + 1, y + 1] = 0.4 * u_ref[1, x + 2, y + 2] + i


def inner_kernel(start, shots, cell_in, amp_in, raw_ref, k2_in, u_ref, v_ref, e_ref, cb_ref, w_ref, cw_ref, cell_ref, amp_ref, k2_ref, held_ref, sems):
    rows = [pl.ds(part * (B * B // 4), B * B // 4) for part in range(4)]
    pairs = [(cell_in, cell_ref), (amp_in, amp_ref), (k2_in, k2_ref)]
    pairs += [(raw_ref.at[:, pl.ds(start, shots), at], held_ref.at[:, :, at]) for at in rows]
    copies = start_all(small_copies(pairs, sems))
    for copy in copies[:3]:
        copy.wait()
    row, column = place()
    source = sources(cell_ref, amp_ref, start, shots)
    raw = held_ref.reshape(2, shots * STRIDE, Z)

    def first(x):
        cw_r, cw_i = weight(coarse_k(k2_ref, x), 3.0)
        cw_ref[0, x] = cw_r
        cw_ref[1, x] = cw_i
        for half in range(2):
            w_r, w_i = weight(k2_ref[2 * x + half], 6.0)
            w_ref[0, 2 * x + half + 1, pl.ds(1, B), :] = w_r
            w_ref[1, 2 * x + half + 1, pl.ds(1, B), :] = w_i
        for y in range(C):
            total = [None, None]
            for half in range(2):
                for other in range(2):
                    fx, fy = 2 * x + half, 2 * y + other
                    r, i = (raw[c, pl.ds(fx * B + fy, shots, stride=STRIDE), :] for c in range(2))
                    r, i = with_source(source, row, column, fx, fy, r, i)
                    total = [r, i] if total[0] is None else [total[0] + r, total[1] + i]
                    w_r = row_of(w_ref, 0, fx + 1, fy + 1, shots)
                    w_i = row_of(w_ref, 1, fx + 1, fy + 1, shots)
                    r, i = times(w_r, w_i, r, i)
                    u_ref[0, fx + 2, fy + 2] = r
                    u_ref[1, fx + 2, fy + 2] = i
            cb_ref[0, x, y] = 0.01 * total[0]
            cb_ref[1, x, y] = 0.01 * total[1]

    for part in range(4):
        copies[3 + part].wait()
        pl.loop(2 * part, 2 * part + 2)(first)

    @pl.loop(1, B - 1, unroll=2)
    def _(x):
        second_v(shots, u_ref, w_ref, v_ref, [(x, y) for y in range(1, B - 1)])

    @pl.loop(1, C - 1, unroll=3)
    def _(x):
        first_coarse(shots, v_ref, cb_ref, cw_ref, e_ref, [(x, y) for y in range(1, C - 1)])


def y_faces_kernel(start, shots, x0_ref, x1_ref, u_ref, k2_ref, y0_ref, y1_ref):
    row, column = place()
    even = row % 2 == 0
    flag = column % 2
    base = 68 * shots
    coarse_base = 64 * shots + B
    for out, high in ((y0_ref, flag == 0), (y1_ref, flag == 1)):
        y = jnp.where(high, B - 1, 0)
        for c in range(2):
            at = pl.ds(pl.multiple_of((y * 2 + c) * shots, 8), shots)
            first, second = x0_ref[at, :], x1_ref[at, :]
            out[pl.ds(c * shots, shots), :] = jnp.where(even, second, first)
            out[pl.ds((17 * 2 + c) * shots, shots), :] = jnp.where(even, first, second)
        for d in range(2):
            from_y = jnp.where(high, B - 1 - d, d) + 2
            at = 1 if d == 0 else 18
            for x in range(B):
                for c in range(2):
                    out[pl.ds(((at + x) * 2 + c) * shots, shots), :] = u_ref[c, x + 2, from_y]
        if start > 0:
            continue
        out[pl.ds(base, B), :] = jnp.where(high, k2_ref[:, B - 1, :], k2_ref[:, 0, :])
        rows = [coarse_k(k2_ref, x) for x in range(C)]
        for d in range(3):
            at = base + B + d * 16
            for h in range(3):
                first = x0_ref[pl.ds(coarse_base + h * C, C), :]
                second = x1_ref[pl.ds(coarse_base + h * C, C), :]
                for position, halo in ((2 - h, jnp.where(even, second, first)), (11 + h, jnp.where(even, first, second))):
                    out[pl.ds(at + position, 1), :] = jnp.where(high, halo[C - 1 - d : C - d], halo[d : d + 1])
            for x in range(C):
                out[pl.ds(at + 3 + x, 1), :] = jnp.where(high, rows[x][C - 1 - d : C - d], rows[x][d : d + 1])
            out[pl.ds(at + 14, 2), :] = jnp.zeros((2, Z), F32)


def ring_kernel(start, shots, x0_ref, x1_ref, y0_ref, y1_ref, cb_ref, cw_ref, u_in, v_in, e_in, w_in, u_ref, v_ref, e_ref, w_ref, ex0_ref, ex1_ref):
    del u_in, v_in, e_in, w_in
    row, column = place()
    flag_x, flag_y = row % 2, column % 2
    for message, high in ((x0_ref, flag_x == 0), (x1_ref, flag_x == 1)):
        for d in range(2):
            to = jnp.where(high, B + 2 + d, 1 - d)
            for y in range(B):
                for c in range(2):
                    u_ref[c, to, y + 2] = message[pl.ds(((d * B + y) * 2 + c) * shots, shots), :]
        if start > 0:
            continue
        w_r, w_i = weight(message[pl.ds(64 * shots, B), :], 6.0)
        to = jnp.where(high, B + 1, 0)
        w_ref[0, to, pl.ds(1, B), :] = w_r
        w_ref[1, to, pl.ds(1, B), :] = w_i
    for message, high in ((y0_ref, flag_y == 0), (y1_ref, flag_y == 1)):
        for d in range(2):
            to = jnp.where(high, B + 2 + d, 1 - d)
            at, first, count = ((0, 1, 18), (18, 2, 16))[d]
            for x in range(count):
                for c in range(2):
                    u_ref[c, first + x, to] = message[pl.ds(((at + x) * 2 + c) * shots, shots), :]
        if start > 0:
            continue
        w_r, w_i = weight(message[pl.ds(68 * shots, B), :], 6.0)
        to = jnp.where(high, B + 1, 0)
        for x in range(B):
            w_ref[0, x + 1, pl.ds(to, 1), :] = w_r[x : x + 1]
            w_ref[1, x + 1, pl.ds(to, 1), :] = w_i[x : x + 1]

    @pl.loop(0, B, unroll=UNROLL)
    def _(y):
        second_v(shots, u_ref, w_ref, v_ref, [(x, y) for x in (-1, 0, B - 1, B)])

    @pl.loop(0, B, unroll=UNROLL)
    def _(x):
        second_v(shots, u_ref, w_ref, v_ref, [(x, y) for y in (-1, 0, B - 1, B)])

    @pl.loop(0, C, unroll=UNROLL)
    def _(y):
        first_coarse(shots, v_ref, cb_ref, cw_ref, e_ref, [(x, y) for x in (0, C - 1)])

    @pl.loop(1, C - 1, unroll=3)
    def _(x):
        first_coarse(shots, v_ref, cb_ref, cw_ref, e_ref, [(x, y) for y in (0, C - 1)])

    for out, high in ((ex0_ref, flag_x == 0), (ex1_ref, flag_x == 1)):
        for d in range(4):
            x = jnp.where(high, C - 1 - d, d) + 4
            for y in range(C):
                for c in range(2):
                    out[pl.ds(((d * C + y) * 2 + c) * shots, shots), :] = e_ref[c, x, y + 4]


def weights_kernel(shots, x0_ref, x1_ref, y0_ref, y1_ref, k2_ref, cwh_ref):
    row, column = place()
    flag_x, flag_y = row % 2, column % 2
    for x in range(C):
        cw_r, cw_i = weight(coarse_k(k2_ref, x), 3.0)
        cwh_ref[0, x + 3, pl.ds(3, C), :] = cw_r
        cwh_ref[1, x + 3, pl.ds(3, C), :] = cw_i
    for message, high in ((x0_ref, flag_x == 0), (x1_ref, flag_x == 1)):
        for d in range(3):
            to = jnp.where(high, C + 3 + d, 2 - d)
            cw_r, cw_i = weight(message[pl.ds(64 * shots + B + d * C, C), :], 3.0)
            cwh_ref[0, to, pl.ds(3, C), :] = cw_r
            cwh_ref[1, to, pl.ds(3, C), :] = cw_i
    for message, high in ((y0_ref, flag_y == 0), (y1_ref, flag_y == 1)):
        for d in range(3):
            to = jnp.where(high, C + 3 + d, 2 - d)
            cw_r, cw_i = weight(message[pl.ds(68 * shots + B + d * 16, 16), :], 3.0)
            for x in range(14):
                cwh_ref[0, x, pl.ds(to, 1), :] = cw_r[x : x + 1]
                cwh_ref[1, x, pl.ds(to, 1), :] = cw_i[x : x + 1]


def base_kernel(shots, u_ref, v_ref, w_ref, g_ref):
    @pl.loop(0, B, unroll=2)
    def _(x):
        sums = near(v_ref, [(x + 1, y + 1) for y in range(B)])
        for y, (r, i) in enumerate(sums):
            r, i = times(row_of(w_ref, 0, x + 1, y + 1, shots), row_of(w_ref, 1, x + 1, y + 1, shots), r, i)
            g_ref[0, x, y] = v_ref[0, x + 1, y + 1] + 0.84 * u_ref[0, x + 2, y + 2] + r
            g_ref[1, x, y] = v_ref[1, x + 1, y + 1] + 0.84 * u_ref[1, x + 2, y + 2] + i


def coarse_y_kernel(shots, ex0_ref, ex1_ref, e_in, e_ref, ey0_ref, ey1_ref):
    del e_in
    row, column = place()
    flag_x, flag_y = row % 2, column % 2
    for message, high in ((ex0_ref, flag_x == 0), (ex1_ref, flag_x == 1)):
        for d in range(4):
            to = jnp.where(high, C + 4 + d, 3 - d)
            for y in range(C):
                for c in range(2):
                    e_ref[c, to, y + 4] = message[pl.ds(((d * C + y) * 2 + c) * shots, shots), :]
    for out, high in ((ey0_ref, flag_y == 0), (ey1_ref, flag_y == 1)):
        for d in range(4):
            y = jnp.where(high, C - 1 - d, d) + 4
            for n in range(Y_COUNT[d]):
                for c in range(2):
                    out[pl.ds(((Y_START[d] + n) * 2 + c) * shots, shots), :] = e_ref[c, 1 + d + n, y]


def final_kernel(start, shots, ey0_ref, ey1_ref, cwh_ref, w_ref, g_ref, *refs):
    e_ref, out_ref, e2_ref, e3_ref, stage_ref, sems = refs[-6:]
    row, column = place()
    flag_y = column % 2
    for message, high in ((ey0_ref, flag_y == 0), (ey1_ref, flag_y == 1)):
        for d in range(4):
            to = jnp.where(high, C + 4 + d, 3 - d)
            for n in range(Y_COUNT[d]):
                for c in range(2):
                    e_ref[c, 1 + d + n, to] = message[pl.ds(((Y_START[d] + n) * 2 + c) * shots, shots), :]
    stage = stage_ref.reshape(2, shots * STRIDE, Z)

    def sweep(old, new, x, reach_y):
        cells = range(-reach_y, C + reach_y)
        along = [z_sum(old[c, x + 4, y + 4]) for y in cells for c in range(2)]
        for n, y in enumerate(cells):
            parts = []
            for c in range(2):
                sides = (old[c, x + 3, y + 4] + old[c, x + 5, y + 4]) + (old[c, x + 4, y + 3] + old[c, x + 4, y + 5])
                parts.append(0.25 * sides + along[2 * n + c])
            w_r, w_i = row_of(cwh_ref, 0, x + 3, y + 3, shots), row_of(cwh_ref, 1, x + 3, y + 3, shots)
            parts = times(w_r, w_i, *parts)
            for c in range(2):
                new[c, x + 4, y + 4] = 0.2 * old[c, x + 4, y + 4] + e_ref[c, x + 4, y + 4] + parts[c]

    for old, new, reach in ((e_ref, e2_ref, 3), (e2_ref, e3_ref, 2), (e3_ref, e2_ref, 1)):

        @pl.loop(0, C, unroll=UNROLL)
        def _(x, old=old, new=new, reach=reach):
            sweep(old, new, x, reach)

        for d in range(1, reach + 1):
            for x in (-d, C - 1 + d):
                sweep(old, new, x, reach - d)

    def finish(x):
        along = [z_sum(e2_ref[c, x + 4, y + 4]) for y in range(C) for c in range(2)]
        for y in range(C):
            e = [e2_ref[c, x + 4, y + 4] for c in range(2)]
            near_x = [[e2_ref[c, x + 3 + 2 * half, y + 4] for c in range(2)] for half in range(2)]
            near_y = [[e2_ref[c, x + 4, y + 3 + 2 * half] for c in range(2)] for half in range(2)]
            middle = [2.0 * e[c] + along[2 * y + c] for c in range(2)]
            for half in range(2):
                total = [middle[c] + near_x[half][c] for c in range(2)]
                for other in range(2):
                    fx, fy = 2 * x + half, 2 * y + other
                    w_r, w_i = row_of(w_ref, 0, fx + 1, fy + 1, shots), row_of(w_ref, 1, fx + 1, fy + 1, shots)
                    change = times(w_r, w_i, total[0] + near_y[other][0], total[1] + near_y[other][1])
                    for c in range(2):
                        value = g_ref[c, fx, fy] + 0.2 * e[c] + change[c]
                        stage[c, pl.ds(fx * B + fy, shots, stride=STRIDE), :] = value

    copies = []
    for part in range(PARTS):
        width = C // PARTS
        pl.loop(part * width, (part + 1) * width, unroll=min(UNROLL, width))(finish)
        rows = pl.ds(part * (B * B // PARTS), B * B // PARTS)
        copy = pltpu.make_async_copy(stage_ref.at[:, :, rows], out_ref.at[:, pl.ds(start, shots), rows], sems.at[part])
        copy.start()
        copies.append(copy)
    for copy in copies:
        copy.wait()


def call(kernel, inputs, outs, *, aliases={}, scratch=(), limit=16, flops=1, moved=1, out_any=()):
    spaces = {"h": pltpu.HBM, "r": pltpu.VMEM}
    return pl.pallas_call(
        kernel,
        in_specs=[pl.BlockSpec(memory_space=spaces[kind]) for kind, _ in inputs],
        out_specs=[pl.BlockSpec(memory_space=spaces["h" if n in out_any else "r"]) for n in range(len(outs))],
        out_shape=[jax.ShapeDtypeStruct(shape, F32) if n in out_any else pltpu.VMEM(shape, F32) for n, shape in enumerate(outs)],
        input_output_aliases=aliases,
        scratch_shapes=list(scratch),
        compiler_params=pltpu.CompilerParams(vmem_limit_bytes=limit * 1024 * 1024),
        cost_estimate=pl.CostEstimate(flops=flops, bytes_accessed=moved, transcendentals=0),
    )(*[pltpu.with_memory_space_constraint(value, spaces[kind]) for kind, value in inputs])


def swaps(pairs):
    return [pair for a, b in pairs for pair in ((a, b), (b, a))]


X0 = swaps([(t, t + TY) for t in range(16) if (t // TY) % 2 == 0])
X1 = swaps([(t, t + TY) for t in range(TY, 2 * TY)])
Y0 = swaps([(t, t + 1) for t in range(0, 16, 2)])
Y1 = swaps([(t, t + 1) for t in range(1, 16, TY)])


def swap(first, first_pairs, second, second_pairs):
    first = lax.ppermute(first, "space", first_pairs)
    second = lax.ppermute(second, "space", second_pairs)
    return first, second


SHOTS = 8
dma = pltpu.SemaphoreType.DMA
U_SHAPE = (2, B + 4, B + 4, SHOTS, Z)
V_SHAPE = (2, B + 2, B + 2, SHOTS, Z)
W_SHAPE = (2, B + 2, B + 2, Z)
E_SHAPE = (2, 2 * C, 2 * C, SHOTS, Z)
part = functools.partial


def small(total):
    return [pltpu.SMEM((total,), jnp.int32), pltpu.SMEM((2, total), F32), pltpu.VMEM((B, B, Z), F32)]


def faces(start, raw, k2, cell, amp):
    return call(
        part(faces_kernel, start, SHOTS),
        [("h", cell), ("h", amp), ("h", raw), ("h", k2)],
        [(64 * SHOTS + (0 if start else 40), Z)] * 2,
        scratch=small(cell.shape[0]) + [pltpu.VMEM((2, SHOTS, FACE_STRIDE, Z), F32)] * 2 + [dma((5,))],
    )


def inner(start, raw, k2, cell, amp):
    return call(
        part(inner_kernel, start, SHOTS),
        [("h", cell), ("h", amp), ("h", raw), ("h", k2)],
        [U_SHAPE, V_SHAPE, E_SHAPE, (2, C, C, SHOTS, Z), W_SHAPE, (2, C, C, Z)],
        scratch=small(cell.shape[0]) + [pltpu.VMEM((2, SHOTS, STRIDE, Z), F32), dma((7,))],
    )


def y_faces(start, x0, x1, u, k2):
    return call(
        part(y_faces_kernel, start, SHOTS),
        [("r", x0), ("r", x1), ("r", u), ("r", k2)],
        [(68 * SHOTS + (0 if start else 64), Z)] * 2,
    )


def ring(start, x0, x1, y0, y1, cb, cw, u, v, e, w):
    inputs = [("r", value) for value in (x0, x1, y0, y1, cb, cw, u, v, e, w)]
    return call(
        part(ring_kernel, start, SHOTS),
        inputs,
        [U_SHAPE, V_SHAPE, E_SHAPE, W_SHAPE, (64 * SHOTS, Z), (64 * SHOTS, Z)],
        aliases={6: 0, 7: 1, 8: 2, 9: 3},
    )


def weights(x0, x1, y0, y1, k2):
    inputs = [("r", value) for value in (x0, x1, y0, y1, k2)]
    return call(part(weights_kernel, SHOTS), inputs, [(2, 14, 14, Z)])[0]


def base(u, v, w):
    return call(part(base_kernel, SHOTS), [("r", u), ("r", v), ("r", w)], [(2, B, B, SHOTS, Z)])[0]


def coarse_y(ex0, ex1, e):
    return call(
        part(coarse_y_kernel, SHOTS),
        [("r", ex0), ("r", ex1), ("r", e)],
        [E_SHAPE, (88 * SHOTS, Z), (88 * SHOTS, Z)],
        aliases={2: 0},
    )


def final(start, ey0, ey1, cwh, w, g, e, out):
    total = 2 * SHOTS
    inputs = [("r", value) for value in (ey0, ey1, cwh, w, g, e)] + ([] if out is None else [("h", out)])
    return call(
        part(final_kernel, start, SHOTS),
        inputs,
        [E_SHAPE, (2, total, B * B, Z)],
        aliases={5: 0} if out is None else {5: 0, 6: 1},
        out_any=(1,),
        scratch=[pltpu.VMEM(E_SHAPE, F32), pltpu.VMEM(E_SHAPE, F32), pltpu.VMEM((2, SHOTS, STRIDE, Z), F32), dma((PARTS,))],
    )[1]


def after(value, *others):
    return lax.optimization_barrier((value, *others))[0]


def shards(right_side, wavenumber_sq, source_cell, source_amplitude):
    shots = right_side.shape[1]
    raw = right_side.reshape(2, shots, B * B, Z)
    k2 = wavenumber_sq[0]
    args = (raw, k2, source_cell, source_amplitude)
    xs = [swap(*pair_of(faces(start, *args), X0, X1)) for start in (0, SHOTS)]
    us, vs, es, cbs, ws, cws = zip(*[inner(start, *args) for start in (0, SHOTS)])
    xs[0] = after(xs[0], us[1])
    ys = [swap(*pair_of(y_faces(n * SHOTS, *xs[n], us[n], k2), Y0, Y1)) for n in range(2)]
    w = ws[0]
    exs, gs = [], []
    es = list(es)
    cwh = weights(*xs[0], *ys[0], k2)
    for n in range(2):
        u, v, es[n], w, *ex = ring(n * SHOTS, *xs[n], *ys[n], cbs[n], cws[0], us[n], vs[n], es[n], w)
        exs.append(swap(*pair_of(ex, X0, X1)))
        gs.append((u, v))
    gs = [base(*g, w) for g in gs]
    exs[0] = after(exs[0], *gs)
    eys = []
    for n in range(2):
        es[n], *ey = coarse_y(*exs[n], es[n])
        eys.append(swap(*pair_of(ey, Y0, Y1)))
    out = None
    for n in range(2):
        out = final(n * SHOTS, *eys[n], cwh, w, gs[n], es[n], out)
    return out.reshape(right_side.shape)


def pair_of(values, first_pairs, second_pairs):
    first, second = values
    return first, first_pairs, second, second_pairs


def solution(mesh):
    return jax.shard_map(
        shards,
        mesh=mesh,
        in_specs=(
            P(None, "shot", "space", None, None, None),
            P("space", None, None, None),
            P("shot"),
            P(None, "shot"),
        ),
        out_specs=P(None, "shot", "space", None, None, None),
        check_vma=False,
    )
```

```python
import functools

import jax
import jax.numpy as jnp
from jax import lax
from jax.experimental import pallas as pl
from jax.experimental.pallas import tpu as pltpu
from jax.sharding import PartitionSpec as P

TY = 4
OMEGA = 0.8
BETA = 0.5
B = 16
C = 8
Z = 128
F32 = jnp.float32
UNROLL = 8
PARTS = 2
FACE_STRIDE = 2 * B + 8
STRIDE = B * B + 8
Y_COUNT = (14, 12, 10, 8)
Y_START = (0, 14, 26, 36)


def z_sum(u):
    lane = lax.broadcasted_iota(jnp.int32, u.shape, 1)
    low = jnp.where(lane == 0, 0.0, pltpu.roll(u, 1, 1))
    high = jnp.where(lane == Z - 1, 0.0, pltpu.roll(u, Z - 1, 1))
    return low + high


def weight(k, centre):
    real = centre - k
    imag = BETA * k
    scale = jnp.where(k > 0.0, OMEGA / (real * real + imag * imag), 0.0)
    return real * scale, -imag * scale


def times(w_r, w_i, r, i):
    return w_r * r - w_i * i, w_r * i + w_i * r


def row_of(ref, c, x, y, shots):
    return jnp.broadcast_to(ref[c, x, pl.ds(y, 1), :], (shots, Z))


def sides_of(ref, c, x, y):
    return (ref[c, x - 1, y] + ref[c, x + 1, y]) + (ref[c, x, y - 1] + ref[c, x, y + 1])


def near(ref, cells):
    along = [z_sum(ref[c, x, y]) for x, y in cells for c in range(2)]
    return [[along[2 * n + c] + sides_of(ref, c, x, y) for c in range(2)] for n, (x, y) in enumerate(cells)]


def place():
    tile = lax.axis_index("space")
    return tile // TY, tile % TY


def sources(cell_ref, amp_ref, start, shots):
    sub = lax.broadcasted_iota(jnp.int32, (shots, Z), 0)
    lane = lax.broadcasted_iota(jnp.int32, (shots, Z), 1)
    cell = jnp.zeros((shots, Z), jnp.int32)
    amp_r = jnp.zeros((shots, Z), F32)
    amp_i = jnp.zeros((shots, Z), F32)
    for s in range(shots):
        cell = jnp.where(sub == s, cell_ref[start + s], cell)
        amp_r = jnp.where(sub == s, amp_ref[0, start + s], amp_r)
        amp_i = jnp.where(sub == s, amp_ref[1, start + s], amp_i)
    return cell - lane, amp_r, amp_i


def with_source(source, row, column, x, y, r, i):
    spot, amp_r, amp_i = source
    hit = spot == ((row * B + x) * (TY * B) + column * B + y) * Z
    return r + jnp.where(hit, amp_r, 0.0), i + jnp.where(hit, amp_i, 0.0)


def coarse_k(k2_ref, x):
    total = k2_ref[2 * x, pl.ds(0, C, stride=2), :] + k2_ref[2 * x + 1, pl.ds(0, C, stride=2), :]
    total = total + k2_ref[2 * x, pl.ds(1, C, stride=2), :] + k2_ref[2 * x + 1, pl.ds(1, C, stride=2), :]
    return 0.25 * total


def start_all(copies):
    for copy in copies:
        copy.start()
    return copies


def small_copies(pairs, sems):
    return [pltpu.make_async_copy(source, target, sems.at[n]) for n, (source, target) in enumerate(pairs)]


def faces_kernel(start, shots, cell_in, amp_in, raw_ref, k2_in, x0_ref, x1_ref, cell_ref, amp_ref, k2_ref, low_ref, high_ref, sems):
    width = 2 * B
    mine = pl.ds(start, shots)
    copies = small_copies(
        [
            (raw_ref.at[:, mine, pl.ds(0, width)], low_ref.at[:, :, pl.ds(0, width)]),
            (raw_ref.at[:, mine, pl.ds(B * B - width, width)], high_ref.at[:, :, pl.ds(0, width)]),
            (cell_in, cell_ref),
            (amp_in, amp_ref),
            (k2_in, k2_ref),
        ],
        sems,
    )
    for copy in start_all(copies):
        copy.wait()
    row, column = place()
    even = row % 2 == 0
    source = sources(cell_ref, amp_ref, start, shots)
    base = 64 * shots
    if start == 0:
        k_low, k_high = k2_ref[0], k2_ref[B - 1]
        x0_ref[pl.ds(base, B), :] = jnp.where(even, k_high, k_low)
        x1_ref[pl.ds(base, B), :] = jnp.where(even, k_low, k_high)
        for d in range(3):
            k_low, k_high = coarse_k(k2_ref, d), coarse_k(k2_ref, C - 1 - d)
            x0_ref[pl.ds(base + B + d * C, C), :] = jnp.where(even, k_high, k_low)
            x1_ref[pl.ds(base + B + d * C, C), :] = jnp.where(even, k_low, k_high)
    low = low_ref.reshape(2, shots * FACE_STRIDE, Z)
    high = high_ref.reshape(2, shots * FACE_STRIDE, Z)
    for d in range(2):
        lw_r, lw_i = weight(k2_ref[d], 6.0)
        hw_r, hw_i = weight(k2_ref[B - 1 - d], 6.0)
        for y in range(B):
            values = []
            for side, local, x, w_r, w_i in ((low, d, d, lw_r, lw_i), (high, 1 - d, B - 1 - d, hw_r, hw_i)):
                r, i = (side[c, pl.ds(local * B + y, shots, stride=FACE_STRIDE), :] for c in range(2))
                r, i = with_source(source, row, column, x, y, r, i)
                values.append(times(w_r[y : y + 1], w_i[y : y + 1], r, i))
            for c in range(2):
                at = pl.ds(((d * B + y) * 2 + c) * shots, shots)
                x0_ref[at, :] = jnp.where(even, values[1][c], values[0][c])
                x1_ref[at, :] = jnp.where(even, values[0][c], values[1][c])


def first_coarse(shots, v_ref, cb_ref, cw_ref, e_ref, cells):
    blocks, rings = [], []
    for x, y in cells:
        fx, fy = 2 * x + 1, 2 * y + 1
        for c in range(2):
            blocks.append((v_ref[c, fx, fy] + v_ref[c, fx + 1, fy]) + (v_ref[c, fx, fy + 1] + v_ref[c, fx + 1, fy + 1]))
            ring = (v_ref[c, fx - 1, fy] + v_ref[c, fx - 1, fy + 1]) + (v_ref[c, fx + 2, fy] + v_ref[c, fx + 2, fy + 1])
            rings.append(ring + (v_ref[c, fx, fy - 1] + v_ref[c, fx + 1, fy - 1]) + (v_ref[c, fx, fy + 2] + v_ref[c, fx + 1, fy + 2]))
    along = [z_sum(block) for block in blocks]
    for n, (x, y) in enumerate(cells):
        r, i = (cb_ref[c, x, y] + 0.25 * (2.0 * blocks[2 * n + c] + rings[2 * n + c] + along[2 * n + c]) for c in range(2))
        r, i = times(row_of(cw_ref, 0, x, y, shots), row_of(cw_ref, 1, x, y, shots), r, i)
        e_ref[0, x + 4, y + 4] = r
        e_ref[1, x + 4, y + 4] = i


def second_v(shots, u_ref, w_ref, v_ref, cells):
    sums = near(u_ref, [(x + 2, y + 2) for x, y in cells])
    for (x, y), (r, i) in zip(cells, sums):
        r, i = times(row_of(w_ref, 0, x + 1, y + 1, shots), row_of(w_ref, 1, x + 1, y + 1, shots), r, i)
        v_ref[0, x + 1, y + 1] = 0.4 * u_ref[0, x + 2, y + 2] + r
        v_ref[1, x + 1, y + 1] = 0.4 * u_ref[1, x + 2, y + 2] + i


def inner_kernel(start, shots, cell_in, amp_in, raw_ref, k2_in, u_ref, v_ref, e_ref, cb_ref, w_ref, cw_ref, cell_ref, amp_ref, k2_ref, held_ref, sems):
    rows = [pl.ds(part * (B * B // 4), B * B // 4) for part in range(4)]
    pairs = [(cell_in, cell_ref), (amp_in, amp_ref), (k2_in, k2_ref)]
    pairs += [(raw_ref.at[:, pl.ds(start, shots), at], held_ref.at[:, :, at]) for at in rows]
    copies = start_all(small_copies(pairs, sems))
    for copy in copies[:3]:
        copy.wait()
    row, column = place()
    source = sources(cell_ref, amp_ref, start, shots)
    raw = held_ref.reshape(2, shots * STRIDE, Z)

    def first(x):
        cw_r, cw_i = weight(coarse_k(k2_ref, x), 3.0)
        cw_ref[0, x] = cw_r
        cw_ref[1, x] = cw_i
        for half in range(2):
            w_r, w_i = weight(k2_ref[2 * x + half], 6.0)
            w_ref[0, 2 * x + half + 1, pl.ds(1, B), :] = w_r
            w_ref[1, 2 * x + half + 1, pl.ds(1, B), :] = w_i
        for y in range(C):
            total = [None, None]
            for half in range(2):
                for other in range(2):
                    fx, fy = 2 * x + half, 2 * y + other
                    r, i = (raw[c, pl.ds(fx * B + fy, shots, stride=STRIDE), :] for c in range(2))
                    r, i = with_source(source, row, column, fx, fy, r, i)
                    total = [r, i] if total[0] is None else [total[0] + r, total[1] + i]
                    w_r = row_of(w_ref, 0, fx + 1, fy + 1, shots)
                    w_i = row_of(w_ref, 1, fx + 1, fy + 1, shots)
                    r, i = times(w_r, w_i, r, i)
                    u_ref[0, fx + 2, fy + 2] = r
                    u_ref[1, fx + 2, fy + 2] = i
            cb_ref[0, x, y] = 0.01 * total[0]
            cb_ref[1, x, y] = 0.01 * total[1]

    for part in range(4):
        copies[3 + part].wait()
        pl.loop(2 * part, 2 * part + 2)(first)

    @pl.loop(1, B - 1, unroll=2)
    def _(x):
        second_v(shots, u_ref, w_ref, v_ref, [(x, y) for y in range(1, B - 1)])

    @pl.loop(1, C - 1, unroll=3)
    def _(x):
        first_coarse(shots, v_ref, cb_ref, cw_ref, e_ref, [(x, y) for y in range(1, C - 1)])


def y_faces_kernel(start, shots, x1_ref, x0_ref, u_ref, k2_ref, y0_ref, y1_ref):
    row, column = place()
    even = row % 2 == 0
    flag = column % 2
    base = 68 * shots
    coarse_base = 64 * shots + B
    for out, high in ((y0_ref, flag == 0), (y1_ref, flag == 1)):
        y = jnp.where(high, B - 1, 0)
        for c in range(2):
            at = pl.ds(pl.multiple_of((y * 2 + c) * shots, 8), shots)
            first, second = x0_ref[at, :], x1_ref[at, :]
            out[pl.ds(c * shots, shots), :] = jnp.where(even, second, first)
            out[pl.ds((17 * 2 + c) * shots, shots), :] = jnp.where(even, first, second)
        for d in range(2):
            from_y = jnp.where(high, B - 1 - d, d) + 2
            at = 1 if d == 0 else 18
            for x in range(B):
                for c in range(2):
                    out[pl.ds(((at + x) * 2 + c) * shots, shots), :] = u_ref[c, x + 2, from_y]
        if start > 0:
            continue
        out[pl.ds(base, B), :] = jnp.where(high, k2_ref[:, B - 1, :], k2_ref[:, 0, :])
        rows = [coarse_k(k2_ref, x) for x in range(C)]
        for d in range(3):
            at = base + B + d * 16
            for h in range(3):
                first = x0_ref[pl.ds(coarse_base + h * C, C), :]
                second = x1_ref[pl.ds(coarse_base + h * C, C), :]
                for position, halo in ((2 - h, jnp.where(even, second, first)), (11 + h, jnp.where(even, first, second))):
                    out[pl.ds(at + position, 1), :] = jnp.where(high, halo[C - 1 - d : C - d], halo[d : d + 1])
            for x in range(C):
                out[pl.ds(at + 3 + x, 1), :] = jnp.where(high, rows[x][C - 1 - d : C - d], rows[x][d : d + 1])
            out[pl.ds(at + 14, 2), :] = jnp.zeros((2, Z), F32)


def ring_kernel(start, shots, y1_ref, y0_ref, x1_ref, x0_ref, cb_ref, cw_ref, u_in, v_in, e_in, w_in, u_ref, v_ref, e_ref, w_ref, ex0_ref, ex1_ref):
    del u_in, v_in, e_in, w_in
    row, column = place()
    flag_x, flag_y = row % 2, column % 2
    for message, high in ((x0_ref, flag_x == 0), (x1_ref, flag_x == 1)):
        for d in range(2):
            to = jnp.where(high, B + 2 + d, 1 - d)
            for y in range(B):
                for c in range(2):
                    u_ref[c, to, y + 2] = message[pl.ds(((d * B + y) * 2 + c) * shots, shots), :]
        if start > 0:
            continue
        w_r, w_i = weight(message[pl.ds(64 * shots, B), :], 6.0)
        to = jnp.where(high, B + 1, 0)
        w_ref[0, to, pl.ds(1, B), :] = w_r
        w_ref[1, to, pl.ds(1, B), :] = w_i
    for message, high in ((y0_ref, flag_y == 0), (y1_ref, flag_y == 1)):
        for d in range(2):
            to = jnp.where(high, B + 2 + d, 1 - d)
            at, first, count = ((0, 1, 18), (18, 2, 16))[d]
            for x in range(count):
                for c in range(2):
                    u_ref[c, first + x, to] = message[pl.ds(((at + x) * 2 + c) * shots, shots), :]
        if start > 0:
            continue
        w_r, w_i = weight(message[pl.ds(68 * shots, B), :], 6.0)
        to = jnp.where(high, B + 1, 0)
        for x in range(B):
            w_ref[0, x + 1, pl.ds(to, 1), :] = w_r[x : x + 1]
            w_ref[1, x + 1, pl.ds(to, 1), :] = w_i[x : x + 1]

    @pl.loop(0, B, unroll=4)
    def _(y):
        second_v(shots, u_ref, w_ref, v_ref, [(x, y) for x in (-1, 0, B - 1, B)])

    @pl.loop(0, B, unroll=4)
    def _(x):
        second_v(shots, u_ref, w_ref, v_ref, [(x, y) for y in (-1, 0, B - 1, B)])

    @pl.loop(0, C, unroll=4)
    def _(y):
        first_coarse(shots, v_ref, cb_ref, cw_ref, e_ref, [(x, y) for x in (0, C - 1)])

    @pl.loop(1, C - 1, unroll=3)
    def _(x):
        first_coarse(shots, v_ref, cb_ref, cw_ref, e_ref, [(x, y) for y in (0, C - 1)])

    for out, high in ((ex0_ref, flag_x == 0), (ex1_ref, flag_x == 1)):
        for d in range(4):
            x = jnp.where(high, C - 1 - d, d) + 4
            for y in range(C):
                for c in range(2):
                    out[pl.ds(((d * C + y) * 2 + c) * shots, shots), :] = e_ref[c, x, y + 4]


def weights_kernel(shots, x0_ref, x1_ref, y0_ref, y1_ref, k2_ref, cwh_ref):
    row, column = place()
    flag_x, flag_y = row % 2, column % 2
    for x in range(C):
        cw_r, cw_i = weight(coarse_k(k2_ref, x), 3.0)
        cwh_ref[0, x + 3, pl.ds(3, C), :] = cw_r
        cwh_ref[1, x + 3, pl.ds(3, C), :] = cw_i
    for message, high in ((x0_ref, flag_x == 0), (x1_ref, flag_x == 1)):
        for d in range(3):
            to = jnp.where(high, C + 3 + d, 2 - d)
            cw_r, cw_i = weight(message[pl.ds(64 * shots + B + d * C, C), :], 3.0)
            cwh_ref[0, to, pl.ds(3, C), :] = cw_r
            cwh_ref[1, to, pl.ds(3, C), :] = cw_i
    for message, high in ((y0_ref, flag_y == 0), (y1_ref, flag_y == 1)):
        for d in range(3):
            to = jnp.where(high, C + 3 + d, 2 - d)
            cw_r, cw_i = weight(message[pl.ds(68 * shots + B + d * 16, 16), :], 3.0)
            for x in range(14):
                cwh_ref[0, x, pl.ds(to, 1), :] = cw_r[x : x + 1]
                cwh_ref[1, x, pl.ds(to, 1), :] = cw_i[x : x + 1]


def base_kernel(shots, u_ref, v_ref, w_ref, g_ref):
    @pl.loop(0, B, unroll=2)
    def _(x):
        sums = near(v_ref, [(x + 1, y + 1) for y in range(B)])
        for y, (r, i) in enumerate(sums):
            r, i = times(row_of(w_ref, 0, x + 1, y + 1, shots), row_of(w_ref, 1, x + 1, y + 1, shots), r, i)
            g_ref[0, x, y] = v_ref[0, x + 1, y + 1] + 0.84 * u_ref[0, x + 2, y + 2] + r
            g_ref[1, x, y] = v_ref[1, x + 1, y + 1] + 0.84 * u_ref[1, x + 2, y + 2] + i


def coarse_y_kernel(shots, ex1_ref, ex0_ref, e_in, e_ref, ey0_ref, ey1_ref):
    del e_in
    row, column = place()
    flag_x, flag_y = row % 2, column % 2
    for message, high in ((ex0_ref, flag_x == 0), (ex1_ref, flag_x == 1)):
        for d in range(4):
            to = jnp.where(high, C + 4 + d, 3 - d)
            for y in range(C):
                for c in range(2):
                    e_ref[c, to, y + 4] = message[pl.ds(((d * C + y) * 2 + c) * shots, shots), :]
    for out, high in ((ey0_ref, flag_y == 0), (ey1_ref, flag_y == 1)):
        for d in range(4):
            y = jnp.where(high, C - 1 - d, d) + 4
            for n in range(Y_COUNT[d]):
                for c in range(2):
                    out[pl.ds(((Y_START[d] + n) * 2 + c) * shots, shots), :] = e_ref[c, 1 + d + n, y]


def sweep(shots, cwh_ref, e_ref, old, new, x, cells):
    along = [z_sum(old[c, x + 4, y + 4]) for y in cells for c in range(2)]
    for n, y in enumerate(cells):
        parts = []
        for c in range(2):
            sides = (old[c, x + 3, y + 4] + old[c, x + 5, y + 4]) + (old[c, x + 4, y + 3] + old[c, x + 4, y + 5])
            parts.append(0.25 * sides + along[2 * n + c])
        parts = times(*[row_of(cwh_ref, c, x + 3, y + 3, shots) for c in range(2)], *parts)
        for c in range(2):
            new[c, x + 4, y + 4] = 0.2 * old[c, x + 4, y + 4] + e_ref[c, x + 4, y + 4] + parts[c]


def early_kernel(shots, cwh_ref, e_ref, e2_ref, e3_ref, e4_ref):
    for n, (old, new) in enumerate(((e_ref, e2_ref), (e2_ref, e3_ref), (e3_ref, e4_ref))):
        reach = 3 - n

        @pl.loop(-reach, C + reach, unroll=C // 2 + reach)
        def _(x, old=old, new=new, cells=range(n + 1, C - 1 - n)):
            sweep(shots, cwh_ref, e_ref, old, new, x, cells)


def final_kernel(start, shots, early, ey1_ref, ey0_ref, cwh_ref, w_ref, g_ref, *refs):
    if early:
        e_ref, out_ref, e2_ref, e3_ref, e4_ref, stage_ref, sems = refs[-7:]
    else:
        e_ref, out_ref, e2_ref, e3_ref, stage_ref, sems = refs[-6:]
        e4_ref = e2_ref
    row, column = place()
    flag_y = column % 2
    for message, high in ((ey0_ref, flag_y == 0), (ey1_ref, flag_y == 1)):
        for d in range(4):
            to = jnp.where(high, C + 4 + d, 3 - d)
            for n in range(Y_COUNT[d]):
                for c in range(2):
                    e_ref[c, 1 + d + n, to] = message[pl.ds(((Y_START[d] + n) * 2 + c) * shots, shots), :]
    stage = stage_ref.reshape(2, shots * STRIDE, Z)

    for n, (old, new) in enumerate(((e_ref, e2_ref), (e2_ref, e3_ref), (e3_ref, e4_ref))):
        reach = 3 - n

        def cells(extent):
            every = range(-extent, C + extent)
            return [y for y in every if not (early and n < y < C - 1 - n)]

        @pl.loop(0, C, unroll=UNROLL)
        def _(x, old=old, new=new):
            sweep(shots, cwh_ref, e_ref, old, new, x, cells(reach))

        for d in range(1, reach + 1):
            for x in (-d, C - 1 + d):
                sweep(shots, cwh_ref, e_ref, old, new, x, cells(reach - d))

    def finish(x):
        along = [z_sum(e4_ref[c, x + 4, y + 4]) for y in range(C) for c in range(2)]
        for y in range(C):
            e = [e4_ref[c, x + 4, y + 4] for c in range(2)]
            near_x = [[e4_ref[c, x + 3 + 2 * half, y + 4] for c in range(2)] for half in range(2)]
            near_y = [[e4_ref[c, x + 4, y + 3 + 2 * half] for c in range(2)] for half in range(2)]
            middle = [2.0 * e[c] + along[2 * y + c] for c in range(2)]
            for half in range(2):
                total = [middle[c] + near_x[half][c] for c in range(2)]
                for other in range(2):
                    fx, fy = 2 * x + half, 2 * y + other
                    w_r, w_i = row_of(w_ref, 0, fx + 1, fy + 1, shots), row_of(w_ref, 1, fx + 1, fy + 1, shots)
                    change = times(w_r, w_i, total[0] + near_y[other][0], total[1] + near_y[other][1])
                    for c in range(2):
                        value = g_ref[c, fx, fy] + 0.2 * e[c] + change[c]
                        stage[c, pl.ds(fx * B + fy, shots, stride=STRIDE), :] = value

    copies = []
    for part in range(PARTS):
        width = C // PARTS
        pl.loop(part * width, (part + 1) * width, unroll=min(UNROLL, width))(finish)
        rows = pl.ds(part * (B * B // PARTS), B * B // PARTS)
        copy = pltpu.make_async_copy(stage_ref.at[:, :, rows], out_ref.at[:, pl.ds(start, shots), rows], sems.at[part])
        copy.start()
        copies.append(copy)
    for copy in copies:
        copy.wait()


def call(kernel, inputs, outs, *, aliases={}, scratch=(), limit=16, flops=1, moved=1, out_any=()):
    spaces = {"h": pltpu.HBM, "r": pltpu.VMEM}
    return pl.pallas_call(
        kernel,
        in_specs=[pl.BlockSpec(memory_space=spaces[kind]) for kind, _ in inputs],
        out_specs=[pl.BlockSpec(memory_space=spaces["h" if n in out_any else "r"]) for n in range(len(outs))],
        out_shape=[jax.ShapeDtypeStruct(shape, F32) if n in out_any else pltpu.VMEM(shape, F32) for n, shape in enumerate(outs)],
        input_output_aliases=aliases,
        scratch_shapes=list(scratch),
        compiler_params=pltpu.CompilerParams(vmem_limit_bytes=limit * 1024 * 1024),
        cost_estimate=pl.CostEstimate(flops=flops, bytes_accessed=moved, transcendentals=0),
    )(*[pltpu.with_memory_space_constraint(value, spaces[kind]) for kind, value in inputs])


def swaps(pairs):
    return [pair for a, b in pairs for pair in ((a, b), (b, a))]


X0 = swaps([(t, t + TY) for t in range(16) if (t // TY) % 2 == 0])
X1 = swaps([(t, t + TY) for t in range(TY, 2 * TY)])
Y0 = swaps([(t, t + 1) for t in range(0, 16, 2)])
Y1 = swaps([(t, t + 1) for t in range(1, 16, TY)])


def swap(first, first_pairs, second, second_pairs):
    first = lax.ppermute(first, "space", first_pairs)
    second = lax.ppermute(second, "space", second_pairs)
    return first, second


SHOTS = 8
dma = pltpu.SemaphoreType.DMA
U_SHAPE = (2, B + 4, B + 4, SHOTS, Z)
V_SHAPE = (2, B + 2, B + 2, SHOTS, Z)
W_SHAPE = (2, B + 2, B + 2, Z)
E_SHAPE = (2, 2 * C, 2 * C, SHOTS, Z)
part = functools.partial


def small(total):
    return [pltpu.SMEM((total,), jnp.int32), pltpu.SMEM((2, total), F32), pltpu.VMEM((B, B, Z), F32)]


def faces(start, raw, k2, cell, amp):
    return call(
        part(faces_kernel, start, SHOTS),
        [("h", cell), ("h", amp), ("h", raw), ("h", k2)],
        [(64 * SHOTS + (0 if start else 40), Z)] * 2,
        scratch=small(cell.shape[0]) + [pltpu.VMEM((2, SHOTS, FACE_STRIDE, Z), F32)] * 2 + [dma((5,))],
    )


def inner(start, raw, k2, cell, amp):
    return call(
        part(inner_kernel, start, SHOTS),
        [("h", cell), ("h", amp), ("h", raw), ("h", k2)],
        [U_SHAPE, V_SHAPE, E_SHAPE, (2, C, C, SHOTS, Z), W_SHAPE, (2, C, C, Z)],
        scratch=small(cell.shape[0]) + [pltpu.VMEM((2, SHOTS, STRIDE, Z), F32), dma((7,))],
    )


def y_faces(start, x0, x1, u, k2):
    return call(
        part(y_faces_kernel, start, SHOTS),
        [("r", x1), ("r", x0), ("r", u), ("r", k2)],
        [(68 * SHOTS + (0 if start else 64), Z)] * 2,
    )


def ring(start, x0, x1, y0, y1, cb, cw, u, v, e, w):
    inputs = [("r", value) for value in (y1, y0, x1, x0, cb, cw, u, v, e, w)]
    return call(
        part(ring_kernel, start, SHOTS),
        inputs,
        [U_SHAPE, V_SHAPE, E_SHAPE, W_SHAPE, (64 * SHOTS, Z), (64 * SHOTS, Z)],
        aliases={6: 0, 7: 1, 8: 2, 9: 3},
    )


def weights(x0, x1, y0, y1, k2):
    inputs = [("r", value) for value in (x0, x1, y0, y1, k2)]
    return call(part(weights_kernel, SHOTS), inputs, [(2, 14, 14, Z)])[0]


def base(u, v, w):
    return call(part(base_kernel, SHOTS), [("r", u), ("r", v), ("r", w)], [(2, B, B, SHOTS, Z)])[0]


def coarse_y(ex0, ex1, e):
    return call(
        part(coarse_y_kernel, SHOTS),
        [("r", ex1), ("r", ex0), ("r", e)],
        [E_SHAPE, (88 * SHOTS, Z), (88 * SHOTS, Z)],
        aliases={2: 0},
    )


def early_sweeps(cwh, e):
    return call(part(early_kernel, SHOTS), [("r", cwh), ("r", e)], [E_SHAPE] * 3)


def final(start, ey0, ey1, cwh, w, g, e, out, early=()):
    total = 2 * SHOTS
    inputs = [("r", value) for value in (ey1, ey0, cwh, w, g, e)] + ([] if out is None else [("h", out)])
    aliases = {5: 0} if out is None else {5: 0, 6: 1}
    for n, value in enumerate(early):
        aliases[len(inputs)] = 2 + n
        inputs.append(("r", value))
    return call(
        part(final_kernel, start, SHOTS, len(early) > 0),
        inputs,
        [E_SHAPE, (2, total, B * B, Z)] + [E_SHAPE] * len(early),
        aliases=aliases,
        out_any=(1,),
        scratch=[pltpu.VMEM(E_SHAPE, F32)] * (0 if early else 2) + [pltpu.VMEM((2, SHOTS, STRIDE, Z), F32), dma((PARTS,))],
    )[1]


def after(value, *others):
    return lax.optimization_barrier((value, *others))[0]


def shards(right_side, wavenumber_sq, source_cell, source_amplitude):
    shots = right_side.shape[1]
    raw = right_side.reshape(2, shots, B * B, Z)
    k2 = wavenumber_sq[0]
    args = (raw, k2, source_cell, source_amplitude)
    xs = [swap(*pair_of(faces(start, *args), X0, X1)) for start in (0, SHOTS)]
    us, vs, es, cbs, ws, cws = zip(*[inner(start, *args) for start in (0, SHOTS)])
    xs[0] = after(xs[0], us[1])
    ys = [swap(*pair_of(y_faces(n * SHOTS, *xs[n], us[n], k2), Y0, Y1)) for n in range(2)]
    w = ws[0]
    exs, gs = [], []
    es = list(es)
    cwh = weights(*xs[0], *ys[0], k2)
    for n in range(2):
        u, v, es[n], w, *ex = ring(n * SHOTS, *xs[n], *ys[n], cbs[n], cws[0], us[n], vs[n], es[n], w)
        exs.append(swap(*pair_of(ex, X0, X1)))
        gs.append((u, v))
    gs = [base(*g, w) for g in gs]
    exs[0] = after(exs[0], *gs)
    eys = []
    for n in range(2):
        es[n], *ey = coarse_y(*exs[n], es[n])
        eys.append(swap(*pair_of(ey, Y0, Y1)))
        if n == 0:
            early = early_sweeps(cwh, es[0])
            es[1] = after(es[1], *early)
    out = final(0, *eys[0], cwh, w, gs[0], es[0], None, early)
    out = final(SHOTS, *eys[1], cwh, w, gs[1], es[1], out)
    return out.reshape(right_side.shape)


def pair_of(values, first_pairs, second_pairs):
    first, second = values
    return first, first_pairs, second, second_pairs


def solution(mesh):
    return jax.shard_map(
        shards,
        mesh=mesh,
        in_specs=(
            P(None, "shot", "space", None, None, None),
            P("space", None, None, None),
            P("shot"),
            P(None, "shot"),
        ),
        out_specs=P(None, "shot", "space", None, None, None),
        check_vma=False,
    )
```

```python
import functools

import jax
import jax.numpy as jnp
from jax import lax
from jax.experimental import pallas as pl
from jax.experimental.pallas import tpu as pltpu
from jax.sharding import PartitionSpec as P

TY = 4
OMEGA = 0.8
BETA = 0.5
B = 16
C = 8
Z = 128
F32 = jnp.float32
UNROLL = 8
PARTS = 4
FACE_STRIDE = 2 * B + 8
STRIDE = B * B + 8
Y_COUNT = (14, 12, 10, 8)
Y_START = (0, 14, 26, 36)


def z_sum(u):
    lane = lax.broadcasted_iota(jnp.int32, u.shape, 1)
    low = jnp.where(lane == 0, 0.0, pltpu.roll(u, 1, 1))
    high = jnp.where(lane == Z - 1, 0.0, pltpu.roll(u, Z - 1, 1))
    return low + high


def weight(k, centre):
    real = centre - k
    imag = BETA * k
    scale = jnp.where(k > 0.0, OMEGA / (real * real + imag * imag), 0.0)
    return real * scale, -imag * scale


def times(w_r, w_i, r, i):
    return w_r * r - w_i * i, w_r * i + w_i * r


def row_of(ref, c, x, y, shots):
    return jnp.broadcast_to(ref[c, x, pl.ds(y, 1), :], (shots, Z))


def sides_of(ref, c, x, y):
    return (ref[c, x - 1, y] + ref[c, x + 1, y]) + (ref[c, x, y - 1] + ref[c, x, y + 1])


def near(ref, cells):
    along = [z_sum(ref[c, x, y]) for x, y in cells for c in range(2)]
    return [[along[2 * n + c] + sides_of(ref, c, x, y) for c in range(2)] for n, (x, y) in enumerate(cells)]


def place():
    tile = lax.axis_index("space")
    return tile // TY, tile % TY


def sources(cell_ref, amp_ref, start, shots):
    sub = lax.broadcasted_iota(jnp.int32, (shots, Z), 0)
    lane = lax.broadcasted_iota(jnp.int32, (shots, Z), 1)
    cell = jnp.zeros((shots, Z), jnp.int32)
    amp_r = jnp.zeros((shots, Z), F32)
    amp_i = jnp.zeros((shots, Z), F32)
    for s in range(shots):
        cell = jnp.where(sub == s, cell_ref[start + s], cell)
        amp_r = jnp.where(sub == s, amp_ref[0, start + s], amp_r)
        amp_i = jnp.where(sub == s, amp_ref[1, start + s], amp_i)
    return cell - lane, amp_r, amp_i


def with_source(source, row, column, x, y, r, i):
    spot, amp_r, amp_i = source
    hit = spot == ((row * B + x) * (TY * B) + column * B + y) * Z
    return r + jnp.where(hit, amp_r, 0.0), i + jnp.where(hit, amp_i, 0.0)


def coarse_k(k2_ref, x):
    total = k2_ref[2 * x, pl.ds(0, C, stride=2), :] + k2_ref[2 * x + 1, pl.ds(0, C, stride=2), :]
    total = total + k2_ref[2 * x, pl.ds(1, C, stride=2), :] + k2_ref[2 * x + 1, pl.ds(1, C, stride=2), :]
    return 0.25 * total


def start_all(copies):
    for copy in copies:
        copy.start()
    return copies


def small_copies(pairs, sems):
    return [pltpu.make_async_copy(source, target, sems.at[n]) for n, (source, target) in enumerate(pairs)]


def faces_kernel(start, shots, cell_in, amp_in, raw_ref, k2_in, x0_ref, x1_ref, cell_ref, amp_ref, k2_ref, low_ref, high_ref, sems):
    width = 2 * B
    mine = pl.ds(start, shots)
    copies = small_copies(
        [
            (raw_ref.at[:, mine, pl.ds(0, width)], low_ref.at[:, :, pl.ds(0, width)]),
            (raw_ref.at[:, mine, pl.ds(B * B - width, width)], high_ref.at[:, :, pl.ds(0, width)]),
            (cell_in, cell_ref),
            (amp_in, amp_ref),
            (k2_in, k2_ref),
        ],
        sems,
    )
    for copy in start_all(copies):
        copy.wait()
    row, column = place()
    even = row % 2 == 0
    source = sources(cell_ref, amp_ref, start, shots)
    base = 64 * shots
    if start == 0:
        k_low, k_high = k2_ref[0], k2_ref[B - 1]
        x0_ref[pl.ds(base, B), :] = jnp.where(even, k_high, k_low)
        x1_ref[pl.ds(base, B), :] = jnp.where(even, k_low, k_high)
        for d in range(3):
            k_low, k_high = coarse_k(k2_ref, d), coarse_k(k2_ref, C - 1 - d)
            x0_ref[pl.ds(base + B + d * C, C), :] = jnp.where(even, k_high, k_low)
            x1_ref[pl.ds(base + B + d * C, C), :] = jnp.where(even, k_low, k_high)
    low = low_ref.reshape(2, shots * FACE_STRIDE, Z)
    high = high_ref.reshape(2, shots * FACE_STRIDE, Z)
    for d in range(2):
        lw_r, lw_i = weight(k2_ref[d], 6.0)
        hw_r, hw_i = weight(k2_ref[B - 1 - d], 6.0)
        for y in range(B):
            values = []
            for side, local, x, w_r, w_i in ((low, d, d, lw_r, lw_i), (high, 1 - d, B - 1 - d, hw_r, hw_i)):
                r, i = (side[c, pl.ds(local * B + y, shots, stride=FACE_STRIDE), :] for c in range(2))
                r, i = with_source(source, row, column, x, y, r, i)
                values.append(times(w_r[y : y + 1], w_i[y : y + 1], r, i))
            for c in range(2):
                at = pl.ds(((d * B + y) * 2 + c) * shots, shots)
                x0_ref[at, :] = jnp.where(even, values[1][c], values[0][c])
                x1_ref[at, :] = jnp.where(even, values[0][c], values[1][c])


def first_coarse(shots, v_ref, cb_ref, cw_ref, e_ref, cells):
    blocks, rings = [], []
    for x, y in cells:
        fx, fy = 2 * x + 1, 2 * y + 1
        for c in range(2):
            blocks.append((v_ref[c, fx, fy] + v_ref[c, fx + 1, fy]) + (v_ref[c, fx, fy + 1] + v_ref[c, fx + 1, fy + 1]))
            ring = (v_ref[c, fx - 1, fy] + v_ref[c, fx - 1, fy + 1]) + (v_ref[c, fx + 2, fy] + v_ref[c, fx + 2, fy + 1])
            rings.append(ring + (v_ref[c, fx, fy - 1] + v_ref[c, fx + 1, fy - 1]) + (v_ref[c, fx, fy + 2] + v_ref[c, fx + 1, fy + 2]))
    along = [z_sum(block) for block in blocks]
    for n, (x, y) in enumerate(cells):
        r, i = (cb_ref[c, x, y] + 0.25 * (2.0 * blocks[2 * n + c] + rings[2 * n + c] + along[2 * n + c]) for c in range(2))
        r, i = times(row_of(cw_ref, 0, x, y, shots), row_of(cw_ref, 1, x, y, shots), r, i)
        e_ref[0, x + 4, y + 4] = r
        e_ref[1, x + 4, y + 4] = i


def second_v(shots, u_ref, w_ref, v_ref, cells):
    sums = near(u_ref, [(x + 2, y + 2) for x, y in cells])
    for (x, y), (r, i) in zip(cells, sums):
        r, i = times(row_of(w_ref, 0, x + 1, y + 1, shots), row_of(w_ref, 1, x + 1, y + 1, shots), r, i)
        v_ref[0, x + 1, y + 1] = 0.4 * u_ref[0, x + 2, y + 2] + r
        v_ref[1, x + 1, y + 1] = 0.4 * u_ref[1, x + 2, y + 2] + i


def inner_kernel(start, shots, cell_in, amp_in, raw_ref, k2_in, u_ref, v_ref, e_ref, cb_ref, w_ref, cw_ref, cell_ref, amp_ref, k2_ref, held_ref, sems):
    rows = [pl.ds(part * (B * B // 4), B * B // 4) for part in range(4)]
    pairs = [(cell_in, cell_ref), (amp_in, amp_ref), (k2_in, k2_ref)]
    pairs += [(raw_ref.at[:, pl.ds(start, shots), at], held_ref.at[:, :, at]) for at in rows]
    copies = start_all(small_copies(pairs, sems))
    for copy in copies[:3]:
        copy.wait()
    row, column = place()
    source = sources(cell_ref, amp_ref, start, shots)
    raw = held_ref.reshape(2, shots * STRIDE, Z)

    def first(x):
        cw_r, cw_i = weight(coarse_k(k2_ref, x), 3.0)
        cw_ref[0, x] = cw_r
        cw_ref[1, x] = cw_i
        for half in range(2):
            w_r, w_i = weight(k2_ref[2 * x + half], 6.0)
            w_ref[0, 2 * x + half + 1, pl.ds(1, B), :] = w_r
            w_ref[1, 2 * x + half + 1, pl.ds(1, B), :] = w_i
        for y in range(C):
            total = [None, None]
            for half in range(2):
                for other in range(2):
                    fx, fy = 2 * x + half, 2 * y + other
                    r, i = (raw[c, pl.ds(fx * B + fy, shots, stride=STRIDE), :] for c in range(2))
                    r, i = with_source(source, row, column, fx, fy, r, i)
                    total = [r, i] if total[0] is None else [total[0] + r, total[1] + i]
                    w_r = row_of(w_ref, 0, fx + 1, fy + 1, shots)
                    w_i = row_of(w_ref, 1, fx + 1, fy + 1, shots)
                    r, i = times(w_r, w_i, r, i)
                    u_ref[0, fx + 2, fy + 2] = r
                    u_ref[1, fx + 2, fy + 2] = i
            cb_ref[0, x, y] = 0.01 * total[0]
            cb_ref[1, x, y] = 0.01 * total[1]

    for part in range(4):
        copies[3 + part].wait()
        pl.loop(2 * part, 2 * part + 2)(first)

    @pl.loop(1, B - 1, unroll=2)
    def _(x):
        second_v(shots, u_ref, w_ref, v_ref, [(x, y) for y in range(1, B - 1)])

    @pl.loop(1, C - 1, unroll=3)
    def _(x):
        first_coarse(shots, v_ref, cb_ref, cw_ref, e_ref, [(x, y) for y in range(1, C - 1)])


def y_faces_kernel(start, shots, x1_ref, x0_ref, u_ref, k2_ref, y0_ref, y1_ref):
    row, column = place()
    even = row % 2 == 0
    flag = column % 2
    base = 68 * shots
    coarse_base = 64 * shots + B
    for out, high in ((y0_ref, flag == 0), (y1_ref, flag == 1)):
        y = jnp.where(high, B - 1, 0)
        for c in range(2):
            at = pl.ds(pl.multiple_of((y * 2 + c) * shots, 8), shots)
            first, second = x0_ref[at, :], x1_ref[at, :]
            out[pl.ds(c * shots, shots), :] = jnp.where(even, second, first)
            out[pl.ds((17 * 2 + c) * shots, shots), :] = jnp.where(even, first, second)
        for d in range(2):
            from_y = jnp.where(high, B - 1 - d, d) + 2
            at = 1 if d == 0 else 18
            for x in range(B):
                for c in range(2):
                    out[pl.ds(((at + x) * 2 + c) * shots, shots), :] = u_ref[c, x + 2, from_y]
        if start > 0:
            continue
        out[pl.ds(base, B), :] = jnp.where(high, k2_ref[:, B - 1, :], k2_ref[:, 0, :])
        rows = [coarse_k(k2_ref, x) for x in range(C)]
        for d in range(3):
            at = base + B + d * 16
            for h in range(3):
                first = x0_ref[pl.ds(coarse_base + h * C, C), :]
                second = x1_ref[pl.ds(coarse_base + h * C, C), :]
                for position, halo in ((2 - h, jnp.where(even, second, first)), (11 + h, jnp.where(even, first, second))):
                    out[pl.ds(at + position, 1), :] = jnp.where(high, halo[C - 1 - d : C - d], halo[d : d + 1])
            for x in range(C):
                out[pl.ds(at + 3 + x, 1), :] = jnp.where(high, rows[x][C - 1 - d : C - d], rows[x][d : d + 1])
            out[pl.ds(at + 14, 2), :] = jnp.zeros((2, Z), F32)


def ring_kernel(start, shots, y1_ref, y0_ref, x1_ref, x0_ref, cb_ref, cw_ref, u_in, v_in, e_in, w_in, u_ref, v_ref, e_ref, w_ref, ex0_ref, ex1_ref):
    del u_in, v_in, e_in, w_in
    row, column = place()
    flag_x, flag_y = row % 2, column % 2
    for message, high in ((x0_ref, flag_x == 0), (x1_ref, flag_x == 1)):
        for d in range(2):
            to = jnp.where(high, B + 2 + d, 1 - d)
            for y in range(B):
                for c in range(2):
                    u_ref[c, to, y + 2] = message[pl.ds(((d * B + y) * 2 + c) * shots, shots), :]
        if start > 0:
            continue
        w_r, w_i = weight(message[pl.ds(64 * shots, B), :], 6.0)
        to = jnp.where(high, B + 1, 0)
        w_ref[0, to, pl.ds(1, B), :] = w_r
        w_ref[1, to, pl.ds(1, B), :] = w_i
    for message, high in ((y0_ref, flag_y == 0), (y1_ref, flag_y == 1)):
        for d in range(2):
            to = jnp.where(high, B + 2 + d, 1 - d)
            at, first, count = ((0, 1, 18), (18, 2, 16))[d]
            for x in range(count):
                for c in range(2):
                    u_ref[c, first + x, to] = message[pl.ds(((at + x) * 2 + c) * shots, shots), :]
        if start > 0:
            continue
        w_r, w_i = weight(message[pl.ds(68 * shots, B), :], 6.0)
        to = jnp.where(high, B + 1, 0)
        for x in range(B):
            w_ref[0, x + 1, pl.ds(to, 1), :] = w_r[x : x + 1]
            w_ref[1, x + 1, pl.ds(to, 1), :] = w_i[x : x + 1]

    @pl.loop(0, B, unroll=4)
    def _(y):
        second_v(shots, u_ref, w_ref, v_ref, [(x, y) for x in (-1, 0, B - 1, B)])

    @pl.loop(0, B, unroll=4)
    def _(x):
        second_v(shots, u_ref, w_ref, v_ref, [(x, y) for y in (-1, 0, B - 1, B)])

    @pl.loop(0, C, unroll=4)
    def _(y):
        first_coarse(shots, v_ref, cb_ref, cw_ref, e_ref, [(x, y) for x in (0, C - 1)])

    @pl.loop(1, C - 1, unroll=3)
    def _(x):
        first_coarse(shots, v_ref, cb_ref, cw_ref, e_ref, [(x, y) for y in (0, C - 1)])

    for out, high in ((ex0_ref, flag_x == 0), (ex1_ref, flag_x == 1)):
        for d in range(4):
            x = jnp.where(high, C - 1 - d, d) + 4
            for y in range(C):
                for c in range(2):
                    out[pl.ds(((d * C + y) * 2 + c) * shots, shots), :] = e_ref[c, x, y + 4]


def weights_kernel(shots, x0_ref, x1_ref, y0_ref, y1_ref, k2_ref, cwh_ref):
    row, column = place()
    flag_x, flag_y = row % 2, column % 2
    for x in range(C):
        cw_r, cw_i = weight(coarse_k(k2_ref, x), 3.0)
        cwh_ref[0, x + 3, pl.ds(3, C), :] = cw_r
        cwh_ref[1, x + 3, pl.ds(3, C), :] = cw_i
    for message, high in ((x0_ref, flag_x == 0), (x1_ref, flag_x == 1)):
        for d in range(3):
            to = jnp.where(high, C + 3 + d, 2 - d)
            cw_r, cw_i = weight(message[pl.ds(64 * shots + B + d * C, C), :], 3.0)
            cwh_ref[0, to, pl.ds(3, C), :] = cw_r
            cwh_ref[1, to, pl.ds(3, C), :] = cw_i
    for message, high in ((y0_ref, flag_y == 0), (y1_ref, flag_y == 1)):
        for d in range(3):
            to = jnp.where(high, C + 3 + d, 2 - d)
            cw_r, cw_i = weight(message[pl.ds(68 * shots + B + d * 16, 16), :], 3.0)
            for x in range(14):
                cwh_ref[0, x, pl.ds(to, 1), :] = cw_r[x : x + 1]
                cwh_ref[1, x, pl.ds(to, 1), :] = cw_i[x : x + 1]


def base_kernel(shots, u_ref, v_ref, w_ref, g_ref):
    @pl.loop(0, B, unroll=2)
    def _(x):
        sums = near(v_ref, [(x + 1, y + 1) for y in range(B)])
        for y, (r, i) in enumerate(sums):
            r, i = times(row_of(w_ref, 0, x + 1, y + 1, shots), row_of(w_ref, 1, x + 1, y + 1, shots), r, i)
            g_ref[0, x, y] = v_ref[0, x + 1, y + 1] + 0.84 * u_ref[0, x + 2, y + 2] + r
            g_ref[1, x, y] = v_ref[1, x + 1, y + 1] + 0.84 * u_ref[1, x + 2, y + 2] + i


def coarse_y_kernel(shots, ex1_ref, ex0_ref, e_in, e_ref, ey0_ref, ey1_ref):
    del e_in
    row, column = place()
    flag_x, flag_y = row % 2, column % 2
    for message, high in ((ex0_ref, flag_x == 0), (ex1_ref, flag_x == 1)):
        for d in range(4):
            to = jnp.where(high, C + 4 + d, 3 - d)
            for y in range(C):
                for c in range(2):
                    e_ref[c, to, y + 4] = message[pl.ds(((d * C + y) * 2 + c) * shots, shots), :]
    for out, high in ((ey0_ref, flag_y == 0), (ey1_ref, flag_y == 1)):
        for d in range(4):
            y = jnp.where(high, C - 1 - d, d) + 4
            for n in range(Y_COUNT[d]):
                for c in range(2):
                    out[pl.ds(((Y_START[d] + n) * 2 + c) * shots, shots), :] = e_ref[c, 1 + d + n, y]


def sweep(shots, cwh_ref, e_ref, old, new, x, cells):
    along = [z_sum(old[c, x + 4, y + 4]) for y in cells for c in range(2)]
    for n, y in enumerate(cells):
        parts = []
        for c in range(2):
            sides = (old[c, x + 3, y + 4] + old[c, x + 5, y + 4]) + (old[c, x + 4, y + 3] + old[c, x + 4, y + 5])
            parts.append(0.25 * sides + along[2 * n + c])
        parts = times(*[row_of(cwh_ref, c, x + 3, y + 3, shots) for c in range(2)], *parts)
        for c in range(2):
            new[c, x + 4, y + 4] = 0.2 * old[c, x + 4, y + 4] + e_ref[c, x + 4, y + 4] + parts[c]


def early_kernel(shots, cwh_ref, e_ref, e2_ref, e3_ref, e4_ref):
    for n, (old, new) in enumerate(((e_ref, e2_ref), (e2_ref, e3_ref), (e3_ref, e4_ref))):
        reach = 3 - n

        @pl.loop(-reach, C + reach, unroll=C // 2 + reach)
        def _(x, old=old, new=new, cells=range(n + 1, C - 1 - n)):
            sweep(shots, cwh_ref, e_ref, old, new, x, cells)


def final_kernel(start, shots, early, ey1_ref, ey0_ref, cwh_ref, w_ref, g_ref, *refs):
    if early:
        e_ref, out_ref, e2_ref, e3_ref, e4_ref, stage_ref, sems = refs[-7:]
    else:
        e_ref, out_ref, e2_ref, e3_ref, stage_ref, sems = refs[-6:]
        e4_ref = e2_ref
    row, column = place()
    flag_y = column % 2
    for message, high in ((ey0_ref, flag_y == 0), (ey1_ref, flag_y == 1)):
        for d in range(4):
            to = jnp.where(high, C + 4 + d, 3 - d)
            for n in range(Y_COUNT[d]):
                for c in range(2):
                    e_ref[c, 1 + d + n, to] = message[pl.ds(((Y_START[d] + n) * 2 + c) * shots, shots), :]
    stage = stage_ref.reshape(2, shots * STRIDE, Z)

    for n, (old, new) in enumerate(((e_ref, e2_ref), (e2_ref, e3_ref), (e3_ref, e4_ref))):
        reach = 3 - n

        def cells(extent):
            every = range(-extent, C + extent)
            return [y for y in every if not (early and n < y < C - 1 - n)]

        @pl.loop(0, C, unroll=UNROLL)
        def _(x, old=old, new=new):
            sweep(shots, cwh_ref, e_ref, old, new, x, cells(reach))

        for d in range(1, reach + 1):
            for x in (-d, C - 1 + d):
                sweep(shots, cwh_ref, e_ref, old, new, x, cells(reach - d))

    def finish(x):
        along = [z_sum(e4_ref[c, x + 4, y + 4]) for y in range(C) for c in range(2)]
        for y in range(C):
            e = [e4_ref[c, x + 4, y + 4] for c in range(2)]
            near_x = [[e4_ref[c, x + 3 + 2 * half, y + 4] for c in range(2)] for half in range(2)]
            near_y = [[e4_ref[c, x + 4, y + 3 + 2 * half] for c in range(2)] for half in range(2)]
            middle = [2.0 * e[c] + along[2 * y + c] for c in range(2)]
            for half in range(2):
                total = [middle[c] + near_x[half][c] for c in range(2)]
                for other in range(2):
                    fx, fy = 2 * x + half, 2 * y + other
                    w_r, w_i = row_of(w_ref, 0, fx + 1, fy + 1, shots), row_of(w_ref, 1, fx + 1, fy + 1, shots)
                    change = times(w_r, w_i, total[0] + near_y[other][0], total[1] + near_y[other][1])
                    for c in range(2):
                        value = g_ref[c, fx, fy] + 0.2 * e[c] + change[c]
                        stage[c, pl.ds(fx * B + fy, shots, stride=STRIDE), :] = value

    copies = []
    for part in range(PARTS):
        width = C // PARTS
        pl.loop(part * width, (part + 1) * width, unroll=min(UNROLL, width))(finish)
        rows = pl.ds(part * (B * B // PARTS), B * B // PARTS)
        copy = pltpu.make_async_copy(stage_ref.at[:, :, rows], out_ref.at[:, pl.ds(start, shots), rows], sems.at[part])
        copy.start()
        copies.append(copy)
    for copy in copies:
        copy.wait()


def call(kernel, inputs, outs, *, aliases={}, scratch=(), limit=16, flops=1, moved=1, out_any=()):
    spaces = {"h": pltpu.HBM, "r": pltpu.VMEM}
    return pl.pallas_call(
        kernel,
        in_specs=[pl.BlockSpec(memory_space=spaces[kind]) for kind, _ in inputs],
        out_specs=[pl.BlockSpec(memory_space=spaces["h" if n in out_any else "r"]) for n in range(len(outs))],
        out_shape=[jax.ShapeDtypeStruct(shape, F32) if n in out_any else pltpu.VMEM(shape, F32) for n, shape in enumerate(outs)],
        input_output_aliases=aliases,
        scratch_shapes=list(scratch),
        compiler_params=pltpu.CompilerParams(vmem_limit_bytes=limit * 1024 * 1024),
        cost_estimate=pl.CostEstimate(flops=flops, bytes_accessed=moved, transcendentals=0),
    )(*[pltpu.with_memory_space_constraint(value, spaces[kind]) for kind, value in inputs])


def swaps(pairs):
    return [pair for a, b in pairs for pair in ((a, b), (b, a))]


X0 = swaps([(t, t + TY) for t in range(16) if (t // TY) % 2 == 0])
X1 = swaps([(t, t + TY) for t in range(TY, 2 * TY)])
Y0 = swaps([(t, t + 1) for t in range(0, 16, 2)])
Y1 = swaps([(t, t + 1) for t in range(1, 16, TY)])


def swap(first, first_pairs, second, second_pairs):
    first = lax.ppermute(first, "space", first_pairs)
    second = lax.ppermute(second, "space", second_pairs)
    return first, second


SHOTS = 8
dma = pltpu.SemaphoreType.DMA
U_SHAPE = (2, B + 4, B + 4, SHOTS, Z)
V_SHAPE = (2, B + 2, B + 2, SHOTS, Z)
W_SHAPE = (2, B + 2, B + 2, Z)
E_SHAPE = (2, 2 * C, 2 * C, SHOTS, Z)
part = functools.partial


def small(total):
    return [pltpu.SMEM((total,), jnp.int32), pltpu.SMEM((2, total), F32), pltpu.VMEM((B, B, Z), F32)]


def faces(start, raw, k2, cell, amp):
    return call(
        part(faces_kernel, start, SHOTS),
        [("h", cell), ("h", amp), ("h", raw), ("h", k2)],
        [(64 * SHOTS + (0 if start else 40), Z)] * 2,
        scratch=small(cell.shape[0]) + [pltpu.VMEM((2, SHOTS, FACE_STRIDE, Z), F32)] * 2 + [dma((5,))],
    )


def inner(start, raw, k2, cell, amp):
    return call(
        part(inner_kernel, start, SHOTS),
        [("h", cell), ("h", amp), ("h", raw), ("h", k2)],
        [U_SHAPE, V_SHAPE, E_SHAPE, (2, C, C, SHOTS, Z), W_SHAPE, (2, C, C, Z)],
        scratch=small(cell.shape[0]) + [pltpu.VMEM((2, SHOTS, STRIDE, Z), F32), dma((7,))],
    )


def y_faces(start, x0, x1, u, k2):
    return call(
        part(y_faces_kernel, start, SHOTS),
        [("r", x1), ("r", x0), ("r", u), ("r", k2)],
        [(68 * SHOTS + (0 if start else 64), Z)] * 2,
    )


def ring(start, x0, x1, y0, y1, cb, cw, u, v, e, w):
    inputs = [("r", value) for value in (y1, y0, x1, x0, cb, cw, u, v, e, w)]
    return call(
        part(ring_kernel, start, SHOTS),
        inputs,
        [U_SHAPE, V_SHAPE, E_SHAPE, W_SHAPE, (64 * SHOTS, Z), (64 * SHOTS, Z)],
        aliases={6: 0, 7: 1, 8: 2, 9: 3},
    )


def weights(x0, x1, y0, y1, k2):
    inputs = [("r", value) for value in (x0, x1, y0, y1, k2)]
    return call(part(weights_kernel, SHOTS), inputs, [(2, 14, 14, Z)])[0]


def base(u, v, w):
    return call(part(base_kernel, SHOTS), [("r", u), ("r", v), ("r", w)], [(2, B, B, SHOTS, Z)])[0]


def coarse_y(ex0, ex1, e):
    return call(
        part(coarse_y_kernel, SHOTS),
        [("r", ex1), ("r", ex0), ("r", e)],
        [E_SHAPE, (88 * SHOTS, Z), (88 * SHOTS, Z)],
        aliases={2: 0},
    )


def early_sweeps(cwh, e):
    return call(part(early_kernel, SHOTS), [("r", cwh), ("r", e)], [E_SHAPE] * 3)


def final(start, ey0, ey1, cwh, w, g, e, out, early=()):
    total = 2 * SHOTS
    inputs = [("r", value) for value in (ey1, ey0, cwh, w, g, e)] + ([] if out is None else [("h", out)])
    aliases = {5: 0} if out is None else {5: 0, 6: 1}
    for n, value in enumerate(early):
        aliases[len(inputs)] = 2 + n
        inputs.append(("r", value))
    return call(
        part(final_kernel, start, SHOTS, len(early) > 0),
        inputs,
        [E_SHAPE, (2, total, B * B, Z)] + [E_SHAPE] * len(early),
        aliases=aliases,
        out_any=(1,),
        scratch=[pltpu.VMEM(E_SHAPE, F32)] * (0 if early else 2) + [pltpu.VMEM((2, SHOTS, STRIDE, Z), F32), dma((PARTS,))],
    )[1]


def after(value, *others):
    return lax.optimization_barrier((value, *others))[0]


def shards(right_side, wavenumber_sq, source_cell, source_amplitude):
    shots = right_side.shape[1]
    raw = right_side.reshape(2, shots, B * B, Z)
    k2 = wavenumber_sq[0]
    args = (raw, k2, source_cell, source_amplitude)
    xs = [swap(*pair_of(faces(start, *args), X0, X1)) for start in (0, SHOTS)]
    us, vs, es, cbs, ws, cws = zip(*[inner(start, *args) for start in (0, SHOTS)])
    xs[0] = after(xs[0], us[1])
    ys = [swap(*pair_of(y_faces(n * SHOTS, *xs[n], us[n], k2), Y0, Y1)) for n in range(2)]
    w = ws[0]
    exs, gs = [], []
    es = list(es)
    cwh = weights(*xs[0], *ys[0], k2)
    for n in range(2):
        u, v, es[n], w, *ex = ring(n * SHOTS, *xs[n], *ys[n], cbs[n], cws[0], us[n], vs[n], es[n], w)
        exs.append(swap(*pair_of(ex, X0, X1)))
        gs.append((u, v))
    gs = [base(*g, w) for g in gs]
    exs[0] = after(exs[0], *gs)
    eys, early = [], []
    for n in range(2):
        es[n], *ey = coarse_y(*exs[n], es[n])
        eys.append(swap(*pair_of(ey, Y0, Y1)))
        early.append(early_sweeps(cwh, es[n]))
        if n == 0:
            es[1] = after(es[1], *early[0])
    eys[0] = after(eys[0][::-1], *early[1])[::-1]
    out = final(0, *eys[0], cwh, w, gs[0], es[0], None, early[0])
    out = final(SHOTS, *eys[1], cwh, w, gs[1], es[1], out, early[1])
    return out.reshape(right_side.shape)


def pair_of(values, first_pairs, second_pairs):
    first, second = values
    return first, first_pairs, second, second_pairs


def solution(mesh):
    return jax.shard_map(
        shards,
        mesh=mesh,
        in_specs=(
            P(None, "shot", "space", None, None, None),
            P("space", None, None, None),
            P("shot"),
            P(None, "shot"),
        ),
        out_specs=P(None, "shot", "space", None, None, None),
        check_vma=False,
    )
```
